32 devices in a mesh: shot: 2 (over y), col: 16 (over z, x, core).
Axes of the slice: x: 2, y: 2, z: 4, core: 2. Of those that a mesh axis runs over, the one named last changes fastest.
Arguments:
- wave_prev: float32 [256, 64, 512], P(('shot', 'col')), parts along dimension 0, may hold values from -6 to 6
- wave_now: float32 [256, 64, 512], P(('shot', 'col')), parts along dimension 0, may hold values from -6 to 6
- velocity: float32 [256, 64, 512], P(('shot', 'col')), parts along dimension 0, may hold values from 0.03 to 0.2
- source: bfloat16 [2, 256, 64, 512], P(None, ('shot', 'col')), parts along dimension 1, may hold values from -6 to 6
- active: int32 [2, 2048], P(None, ('shot', 'col')), parts along dimension 1, may hold values 0 or 1
- plan: int32 [2048], P(('shot', 'col')), parts along dimension 0, may hold values from 0 to 1023, as said below
- image_in: float32 [2048, 8, 4, 128], P(('shot', 'col')), parts along dimension 0, may hold values from -6 to 6
Outputs:
- wave_first: float32 [256, 64, 512], P(('shot', 'col')), parts along dimension 0
- wave_second: float32 [256, 64, 512], P(('shot', 'col')), parts along dimension 0
- image_out: float32 [2048, 8, 4, 128], P(('shot', 'col')), parts along dimension 0
The draws below stay inside these ranges and needn't reach their ends.
There are 2 independent parts, one for each index of `shot`. The reference program is written for one: setup_inputs(seed, part) draws one part's arguments, and reference() takes and returns one part's arrays. A program takes and returns all parts, laid end to end along the dimension named above; each array names one. Nothing has to cross between parts.
Inputs may be any that keep to these rules, and one draw needn't show every extreme that they name: plan is a permutation of the 1024 brick numbers; the bricks of one device stand in at most 4 slot of any one device, and some pair of devices reaches 4.
All inputs are finite; a program needn't handle non-finite values. No bound on the sum of `active` on one device may be relied on, other than what follows from the above.
Results may differ from the reference program's by a relative error of at most 0.0003.
Values sent between devices are 32-bit elements; how exact they have to be, the bound alone decides.
A program may use at most 64 MiB of HBM per device.

```python
import math
import jax
import jax.numpy as jnp

CX = 8
NY = 64
NZ = 512
BY = 4
BZ = 128
BPD = 64
NB = 1024
NX = 128
N_COL = 16


def draw_plan(key, part):
    key = jax.random.fold_in(key, 7)
    key_pi, key_off, key_sigma, key_rho = jax.random.split(key, 4)
    shuffle = jax.random.permutation(key_pi, N_COL)
    offsets = jax.random.permutation(key_off, N_COL)
    slot_off = offsets[jnp.arange(BPD) % N_COL]
    sigma = jax.random.permutation(key_sigma, BPD)
    rotation = jax.random.randint(key_rho, (N_COL,), 0, BPD)
    target = jnp.arange(N_COL)[:, None]
    anchor = shuffle[(target + slot_off[None, :]) % N_COL]
    local = (sigma[None, :] + rotation[anchor]) % BPD
    return (anchor * BPD + local).reshape(-1).astype(jnp.int32)


def with_ends(result, rng, smallest, top_value):
    longest = result.shape.index(max(result.shape))
    spots = []
    for shift in (0, 1):
        where = [jax.random.randint(jax.random.fold_in(rng, axis), (), 0, length) for axis, length in enumerate(result.shape)]
        where[longest] = (where[longest] + shift) % result.shape[longest]
        spots.append(tuple(where))
    return result.at[spots[0]].set(smallest).at[spots[1]].set(top_value)


def shard_levels(key, shape, pieces, low, top_value):
    level, own = 1.0, jax.random.fold_in(key, 6)
    for axis_at, blocks in pieces:
        steps = jnp.exp(jax.random.uniform(jax.random.fold_in(own, axis_at), (blocks,), jnp.float32, low / len(pieces), top_value / len(pieces)))
        level = level * jnp.repeat(steps, shape[axis_at] // blocks).reshape([-1 if axis == axis_at else 1 for axis in range(len(shape))])
    return level


def gaussian(key, shape, width, bound, pieces=(), dtype=jnp.bfloat16):
    values = jax.random.normal(key, shape, jnp.float32) * width
    if len(pieces) > 0:
        values = shard_levels(key, shape, pieces, -0.22, 0.18) * values
    return jnp.clip(values, min=-bound, max=bound).astype(dtype)


def setup_inputs(seed: int = 0, part: int = 0) -> dict:
    seeds = jax.random.split(jax.random.key(seed), 8)
    own_keys = jax.random.split(jax.random.fold_in(seeds[7], part), 8)
    wave_prev = gaussian(own_keys[0], (NX, NY, NZ), 1.0, 6.0, ((0, 16),), jnp.float32)
    wave_now = gaussian(own_keys[1], (NX, NY, NZ), 1.0, 6.0, ((0, 16),), jnp.float32)
    velocity = jnp.clip(jnp.exp(math.log(0.2) - 1.89712 * jax.random.uniform(own_keys[2], (NX, NY, NZ), jnp.float32) ** shard_levels(own_keys[2], (NX, NY, NZ), ((0, 16),), -0.2, 0.2)), 0.03, 0.2)
    source = gaussian(own_keys[3], (2, NX, NY, NZ), 1.0, 6.0, ((1, 16),))
    active = with_ends((jax.random.randint(own_keys[4], (2, NB), 0, 4) < 3).astype(jnp.int32), jax.random.fold_in(own_keys[4], 1), 0, 1)
    plan = draw_plan(jax.random.fold_in(jax.random.fold_in(seeds[7], part), 71), part)
    image_in = gaussian(own_keys[6], (NB, CX, BY, BZ), 1.0, 6.0, ((0, 16),), jnp.float32)
    return dict(wave_prev=wave_prev, wave_now=wave_now, velocity=velocity, source=source, active=active, plan=plan, image_in=image_in)


STENCIL_COEF = (-205.0 / 72.0, 8.0 / 5.0, -1.0 / 5.0, 8.0 / 315.0, -1.0 / 560.0)


def laplace(field):
    framed = jnp.pad(field, 4)
    size_x, size_y, size_z = field.shape
    summed = (3.0 * STENCIL_COEF[0]) * field
    for radius in range(1, 5):
        summed = summed + STENCIL_COEF[radius] * (
            framed[4 + radius:4 + radius + size_x, 4:4 + size_y, 4:4 + size_z]
            + framed[4 - radius:4 - radius + size_x, 4:4 + size_y, 4:4 + size_z]
            + framed[4:4 + size_x, 4 + radius:4 + radius + size_y, 4:4 + size_z]
            + framed[4:4 + size_x, 4 - radius:4 - radius + size_y, 4:4 + size_z]
            + framed[4:4 + size_x, 4:4 + size_y, 4 + radius:4 + radius + size_z]
            + framed[4:4 + size_x, 4:4 + size_y, 4 - radius:4 - radius + size_z])
    return summed


def mask_of(flags):
    grid = flags.astype(jnp.float32).reshape(N_COL, NY // BY, NZ // BZ)
    spread = jnp.repeat(jnp.repeat(grid, BY, axis=1), BZ, axis=2)
    return jnp.broadcast_to(spread[:, None], (N_COL, CX, NY, NZ)).reshape(NX, NY, NZ)


def reference(wave_prev, wave_now, velocity, source, active, plan, image_in):
    wave_first = mask_of(active[0]) * (2.0 * wave_now - wave_prev + velocity * laplace(wave_now))
    wave_second = mask_of(active[1]) * (2.0 * wave_first - wave_now + velocity * laplace(wave_first))
    increment = source[0].astype(jnp.float32) * wave_first + source[1].astype(jnp.float32) * wave_second
    blocks = increment.reshape(N_COL, CX, NY // BY, BY, NZ // BZ, BZ)
    blocks = blocks.transpose(0, 2, 4, 1, 3, 5).reshape(NB, CX, BY, BZ)
    image_out = image_in + blocks[plan]
    return wave_first, wave_second, image_out
```

```python
import functools

import jax
import jax.numpy as jnp
from jax import lax
from jax.experimental import pallas as pl
from jax.experimental.pallas import tpu as pltpu
from jax.sharding import PartitionSpec as P

COEF = (-205.0 / 72.0, 8.0 / 5.0, -1.0 / 5.0, 8.0 / 315.0, -1.0 / 560.0)
MESH = pl.DeviceIdType.MESH
R = 4
PAD = 8
CH = 16
LANES = 128


def flipped(me, k, bits):
    out = me
    for b in range(bits):
        out = out + ((k // 2**b) % 2) * (2**b) * (1 - 2 * ((me // 2**b) % 2))
    return out


def kernel(
    n, cap, prev_h, now_h, vel_h, src_h, img_h, active_s, place_s, want_v,
    first_h, second_h, out_h,
    x1, x2, acc, prev_v, vel_v, src_v, img_v, second_v, bricks, outgoing, incoming, asked_v, asked_s,
    in_sem, halo_send, halo_recv, ask_send, ask_recv, ask_copy, a2a_send, a2a_recv, out_sem,
):
    me = lax.axis_index("col")
    cx, ny, nz = prev_h.shape
    n_c, n_z = ny // CH, nz // LANES
    slots = place_s.shape[0]
    bits = (n - 1).bit_length()

    def zero_rows(x, _):
        for j in range(n_z):
            for buf in (x1, x2):
                buf[R + x, j, 0:PAD, :] = jnp.zeros((PAD, LANES), jnp.float32)
                buf[R + x, j, PAD + ny : PAD + ny + PAD, :] = jnp.zeros((PAD, LANES), jnp.float32)
        return 0

    own = pl.ds(R, cx)
    body = pl.ds(PAD, ny)
    load_now = [
        pltpu.make_async_copy(
            now_h.at[:, :, pl.ds(j * LANES, LANES)], x1.at[own, j, body, :], in_sem.at[j]
        )
        for j in range(n_z)
    ]
    for copy in load_now:
        copy.start()
    load_prev = pltpu.make_async_copy(prev_h, prev_v, in_sem.at[n_z])
    load_vel = pltpu.make_async_copy(vel_h, vel_v, in_sem.at[n_z + 1])
    load_src = pltpu.make_async_copy(src_h, src_v, in_sem.at[n_z + 2])
    load_img = pltpu.make_async_copy(img_h, img_v, in_sem.at[n_z + 3])
    for copy in (load_prev, load_vel, load_src, load_img):
        copy.start()

    barrier = pltpu.get_barrier_semaphore()

    def greet(k, _):
        pl.semaphore_signal(
            barrier, inc=1, device_id={"col": lax.rem(me + k, n)}, device_id_type=MESH
        )
        return 0

    lax.fori_loop(1, n, greet, 0)

    lax.fori_loop(0, cx, zero_rows, 0)

    def zero_halo(start):
        def plane(x, _):
            for buf in (x1, x2):
                for j in range(n_z):
                    buf[start + x, j, PAD : PAD + ny, :] = jnp.zeros((ny, LANES), jnp.float32)
            return 0

        lax.fori_loop(0, R, plane, 0)

    @pl.when(me == 0)
    def _():
        zero_halo(0)

    @pl.when(me == n - 1)
    def _():
        zero_halo(R + cx)

    for copy in load_now:
        copy.wait()
    pl.semaphore_wait(barrier, n - 1)

    def halo(buf, step, side, c):
        rows = pl.ds(PAD + c * CH, CH)
        source, landing = ((cx, 0), (R, R + cx))[side]
        target = (lax.rem(me + 1, n), lax.rem(me + n - 1, n))[side]
        return pltpu.make_async_remote_copy(
            src_ref=buf.at[pl.ds(source, R), :, rows, :],
            dst_ref=buf.at[pl.ds(landing, R), :, rows, :],
            send_sem=halo_send.at[step, side, c],
            recv_sem=halo_recv.at[step, side, c],
            device_id={"col": target},
            device_id_type=MESH,
        )

    def send_halo(buf, step, c):
        @pl.when(me < n - 1)
        def _():
            halo(buf, step, 0, c).start()

        @pl.when(me > 0)
        def _():
            halo(buf, step, 1, c).start()

    def sent_halo(buf, step, c):
        @pl.when(me < n - 1)
        def _():
            halo(buf, step, 0, c).wait_send()

        @pl.when(me > 0)
        def _():
            halo(buf, step, 1, c).wait_send()

    def take_halo(buf, step, c):
        @pl.when(me > 0)
        def _():
            halo(buf, step, 0, c).wait_recv()

        @pl.when(me < n - 1)
        def _():
            halo(buf, step, 1, c).wait_recv()

    for c in range(n_c):
        send_halo(x1, 0, c)

    def ask(k):
        target = lax.rem(me + k, n)
        return pltpu.make_async_remote_copy(
            src_ref=want_v.at[target],
            dst_ref=asked_v.at[me],
            send_sem=ask_send,
            recv_sem=ask_recv,
            device_id={"col": target},
            device_id_type=MESH,
        )

    def start_ask(k, _):
        ask(k).start()
        return 0

    lax.fori_loop(1, n, start_ask, 0)
    asked_v[me] = want_v[me]

    lane = lax.broadcasted_iota(jnp.int32, (CH, LANES), 1)
    row = lax.broadcasted_iota(jnp.int32, (CH, LANES), 0)

    def along_yz(buf):
        def plane(x, _):
            for c in range(n_c):
                tiles = [buf[R + x, j, PAD + c * CH : PAD + (c + 1) * CH, :] for j in range(n_z)]
                for j in range(n_z):
                    total = (3.0 * COEF[0]) * tiles[j]
                    for r in range(1, R + 1):
                        at = PAD + c * CH
                        pair = buf[R + x, j, at + r : at + r + CH, :] + buf[R + x, j, at - r : at - r + CH, :]
                        up = pltpu.roll(tiles[j], LANES - r, 1)
                        down = pltpu.roll(tiles[j], r, 1)
                        after = pltpu.roll(tiles[j + 1], LANES - r, 1) if j + 1 < n_z else 0.0
                        before = pltpu.roll(tiles[j - 1], r, 1) if j > 0 else 0.0
                        pair = pair + jnp.where(lane < LANES - r, up, after)
                        pair = pair + jnp.where(lane < r, before, down)
                        total = total + COEF[r] * pair
                    acc[x, j, c * CH : (c + 1) * CH, :] = total
            return 0

        lax.fori_loop(0, cx, plane, 0)

    def mask(t, c, j):
        per = CH // 4
        flags = [active_s[t, (c * per + i) * n_z + j].astype(jnp.float32) for i in range(per)]
        out = jnp.full((CH, LANES), flags[per - 1], jnp.float32)
        for i in range(per - 2, -1, -1):
            out = jnp.where(row < 4 * (i + 1), flags[i], out)
        return out

    def following(buf, x, c, j, before, flag):
        rows = slice(PAD + c * CH, PAD + (c + 1) * CH)
        total = acc[x, j, c * CH : (c + 1) * CH, :]
        for r in range(1, R + 1):
            total = total + COEF[r] * (buf[R + x + r, j, rows, :] + buf[R + x - r, j, rows, :])
        here = buf[R + x, j, rows, :]
        speed = vel_v[x, c * CH : (c + 1) * CH, j * LANES : (j + 1) * LANES]
        return here, flag * (2.0 * here - before + speed * total)

    along_yz(x1)
    load_prev.wait()
    load_vel.wait()
    for c in range(n_c):
        take_halo(x1, 0, c)
        flags = [mask(0, c, j) for j in range(n_z)]

        def plane(x, _):
            for j in range(n_z):
                before = prev_v[x, c * CH : (c + 1) * CH, j * LANES : (j + 1) * LANES]
                _, new = following(x1, x, c, j, before, flags[j])
                x2[R + x, j, PAD + c * CH : PAD + (c + 1) * CH, :] = new
            return 0

        lax.fori_loop(0, cx, plane, 0)
        send_halo(x2, 1, c)

    store_first = [
        pltpu.make_async_copy(
            x2.at[own, j, body, :], first_h.at[:, :, pl.ds(j * LANES, LANES)], out_sem.at[j]
        )
        for j in range(n_z)
    ]
    for copy in store_first:
        copy.start()

    along_yz(x2)

    pltpu.make_async_copy(
        asked_v.at[pl.ds(0, n - 1)], asked_v.at[pl.ds(0, n - 1)], ask_recv
    ).wait()
    to_scalar = pltpu.make_async_copy(asked_v, asked_s, ask_copy)
    to_scalar.start()

    load_src.wait()
    for c in range(n_c):
        take_halo(x2, 1, c)
        flags = [mask(1, c, j) for j in range(n_z)]

        def pair(p, _):
            for j in range(n_z):
                gains = []
                for i in range(2):
                    x = 2 * p + i
                    before = x1[R + x, j, PAD + c * CH : PAD + (c + 1) * CH, :]
                    here, new = following(x2, x, c, j, before, flags[j])
                    spot = (slice(c * CH, (c + 1) * CH), slice(j * LANES, (j + 1) * LANES))
                    second_v[(x,) + spot] = new
                    gains.append(
                        src_v[(0, x) + spot].astype(jnp.float32) * here
                        + src_v[(1, x) + spot].astype(jnp.float32) * new
                    )
                for h in range(CH // 8):
                    a, b = (g[h * 8 : (h + 1) * 8, :] for g in gains)
                    low = row[:8] < 4
                    even = jnp.where(low, a, pltpu.roll(b, 4, 0))
                    odd = jnp.where(low, pltpu.roll(a, 4, 0), b)
                    yb = c * (CH // 4) + 2 * h
                    for i, value in enumerate((even, odd)):
                        bricks[(yb + i) * n_z + j, pl.ds(pl.multiple_of(8 * p, 8), 8), :] = value
            return 0

        lax.fori_loop(0, cx // 2, pair, 0)

    to_scalar.wait()

    def pack(dst, at, target):
        for r in range(cap):
            dst[at + r] = bricks[asked_s[target, 0, r]]

    def give(k, target):
        return pltpu.make_async_remote_copy(
            src_ref=outgoing.at[pl.ds(k * cap, cap)],
            dst_ref=incoming.at[pl.ds(me * cap, cap)],
            send_sem=a2a_send,
            recv_sem=a2a_recv,
            device_id={"col": target},
            device_id_type=MESH,
        )

    def partner(k):
        return flipped(me, k, bits) if n == 2**bits else lax.rem(me + k, n)

    def start_give(i, _):
        k = n - 1 - i
        target = partner(k)
        pack(outgoing, k * cap, target)
        give(k, target).start()
        return 0

    lax.fori_loop(0, n - 1, start_give, 0)

    store_second = pltpu.make_async_copy(second_v, second_h, out_sem.at[n_z])
    store_second.start()
    pack(incoming, me * cap, me)
    load_img.wait()

    whole = pl.ds(cap, (n - 1) * cap)
    pltpu.make_async_copy(incoming.at[whole], incoming.at[whole], a2a_recv).wait()
    parts = 4 if slots % 4 == 0 else 1
    per = slots // parts
    stores = []
    for q in range(parts):

        def add(s, _):
            at = q * per + s
            img_v[at] = img_v[at] + incoming[place_s[at]]
            return 0

        lax.fori_loop(0, per, add, 0)
        span = pl.ds(q * per, per)
        copy = pltpu.make_async_copy(img_v.at[span], out_h.at[span], out_sem.at[n_z + 1 + q])
        copy.start()
        stores.append(copy)

    for c in range(n_c):
        sent_halo(x1, 0, c)
        sent_halo(x2, 1, c)
    pltpu.make_async_copy(
        want_v.at[pl.ds(0, n - 1)], want_v.at[pl.ds(0, n - 1)], ask_send
    ).wait()
    pltpu.make_async_copy(outgoing.at[whole], outgoing.at[whole], a2a_send).wait()
    for copy in store_first + [store_second] + stores:
        copy.wait()


def shards(wave_prev, wave_now, velocity, source, active, plan, image_in):
    cx, ny, nz = wave_now.shape
    n = lax.axis_size("col")
    per = plan.shape[0]
    cap = (per + n - 1) // n
    n_c, n_z = ny // CH, nz // LANES

    order = jnp.arange(per, dtype=jnp.int32)
    anchor = lax.div(plan, jnp.int32(per))
    local = plan - anchor * per
    rank = jnp.sum(
        (anchor[None, :] == anchor[:, None]) & (order[None, :] < order[:, None]), axis=1, dtype=jnp.int32
    )
    place = anchor * cap + rank
    device = lax.broadcasted_iota(jnp.int32, (n, 1, LANES, per), 0)
    turn = lax.broadcasted_iota(jnp.int32, (n, 1, LANES, per), 2)
    hit = (anchor[None, None, None, :] == device) & (rank[None, None, None, :] == turn)
    want = jnp.sum(jnp.where(hit, local[None, None, None, :], 0), axis=3, dtype=jnp.int32)

    f32 = jnp.float32
    hbm = pl.BlockSpec(memory_space=pl.ANY)
    smem = pl.BlockSpec(memory_space=pltpu.SMEM)
    vmem = pl.BlockSpec(memory_space=pltpu.VMEM)
    wide = (cx + 2 * R, n_z, ny + 2 * PAD, LANES)
    dma = pltpu.SemaphoreType.DMA
    first, second, image = pl.pallas_call(
        functools.partial(kernel, n, cap),
        out_shape=(
            jax.ShapeDtypeStruct((cx, ny, nz), f32),
            jax.ShapeDtypeStruct((cx, ny, nz), f32),
            jax.ShapeDtypeStruct((per, 32, LANES), f32),
        ),
        in_specs=[hbm] * 5 + [smem, smem, vmem],
        out_specs=(hbm, hbm, hbm),
        scratch_shapes=[
            pltpu.VMEM(wide, f32),
            pltpu.VMEM(wide, f32),
            pltpu.VMEM((cx, n_z, ny, LANES), f32),
            pltpu.VMEM((cx, ny, nz), f32),
            pltpu.VMEM((cx, ny, nz), f32),
            pltpu.VMEM((2, cx, ny, nz), jnp.bfloat16),
            pltpu.VMEM((per, 32, LANES), f32),
            pltpu.VMEM((cx, ny, nz), f32),
            pltpu.VMEM((per, 32, LANES), f32),
            pltpu.VMEM((n * cap, 32, LANES), f32),
            pltpu.VMEM((n * cap, 32, LANES), f32),
            pltpu.VMEM((n, 1, LANES), jnp.int32),
            pltpu.SMEM((n, 1, LANES), jnp.int32),
            dma((n_z + 4,)),
            dma((2, 2, n_c)),
            dma((2, 2, n_c)),
            dma(()),
            dma(()),
            dma(()),
            dma(()),
            dma(()),
            dma((n_z + 5,)),
        ],
        compiler_params=pltpu.CompilerParams(
            collective_id=0, has_side_effects=True, vmem_limit_bytes=40 * 2**20
        ),
    )(
        wave_prev, wave_now, velocity, source, image_in.reshape(per, 32, LANES),
        active, place, want,
    )
    return first, second, image.reshape(image_in.shape)


def solution(mesh):
    lead = ("shot", "col")
    in_specs = (
        P(lead, None, None),
        P(lead, None, None),
        P(lead, None, None),
        P(None, lead, None, None),
        P(None, lead),
        P(lead),
        P(lead, None, None, None),
    )
    out_specs = (P(lead, None, None), P(lead, None, None), P(lead, None, None, None))
    return jax.shard_map(shards, mesh=mesh, in_specs=in_specs, out_specs=out_specs, check_vma=False)
```

```python
import functools

import jax
import jax.numpy as jnp
from jax import lax
from jax.experimental import pallas as pl
from jax.experimental.pallas import tpu as pltpu
from jax.sharding import PartitionSpec as P

COEF = (-205.0 / 72.0, 8.0 / 5.0, -1.0 / 5.0, 8.0 / 315.0, -1.0 / 560.0)
MESH = pl.DeviceIdType.MESH
R = 4
PAD = 8
CH = 16
LANES = 128


def flipped(me, k, bits):
    out = me
    for b in range(bits):
        out = out + ((k // 2**b) % 2) * (2**b) * (1 - 2 * ((me // 2**b) % 2))
    return out


def kernel(
    n, cap, prev_h, now_h, vel_h, src_h, active_s, want_v,
    first_h, second_h, incoming,
    x1, x2, acc, prev_v, vel_v, src_v, second_v, bricks, outgoing, asked_v, asked_s,
    in_sem, halo_send, halo_recv, ask_send, ask_recv, ask_copy, a2a_send, a2a_recv, keep_sem, out_sem,
):
    me = lax.axis_index("col")
    cx, ny, nz = prev_h.shape
    n_c, n_z = ny // CH, nz // LANES
    bits = (n - 1).bit_length()

    def zero_rows(x, _):
        for j in range(n_z):
            for buf in (x1, x2):
                buf[R + x, j, 0:PAD, :] = jnp.zeros((PAD, LANES), jnp.float32)
                buf[R + x, j, PAD + ny : PAD + ny + PAD, :] = jnp.zeros((PAD, LANES), jnp.float32)
        return 0

    own = pl.ds(R, cx)
    body = pl.ds(PAD, ny)
    load_now = [
        pltpu.make_async_copy(
            now_h.at[:, :, pl.ds(j * LANES, LANES)], x1.at[own, j, body, :], in_sem.at[j]
        )
        for j in range(n_z)
    ]
    for copy in load_now:
        copy.start()
    load_prev = pltpu.make_async_copy(prev_h, prev_v, in_sem.at[n_z])
    load_vel = pltpu.make_async_copy(vel_h, vel_v, in_sem.at[n_z + 1])
    load_src = pltpu.make_async_copy(src_h, src_v, in_sem.at[n_z + 2])
    for copy in (load_prev, load_vel, load_src):
        copy.start()

    barrier = pltpu.get_barrier_semaphore()

    def greet(k, _):
        pl.semaphore_signal(
            barrier, inc=1, device_id={"col": lax.rem(me + k, n)}, device_id_type=MESH
        )
        return 0

    lax.fori_loop(1, n, greet, 0)

    lax.fori_loop(0, cx, zero_rows, 0)

    def zero_halo(start):
        def plane(x, _):
            for buf in (x1, x2):
                for j in range(n_z):
                    buf[start + x, j, PAD : PAD + ny, :] = jnp.zeros((ny, LANES), jnp.float32)
            return 0

        lax.fori_loop(0, R, plane, 0)

    @pl.when(me == 0)
    def _():
        zero_halo(0)

    @pl.when(me == n - 1)
    def _():
        zero_halo(R + cx)

    for copy in load_now:
        copy.wait()
    pl.semaphore_wait(barrier, n - 1)

    def halo(buf, step, side, c):
        rows = pl.ds(PAD + c * CH, CH)
        source, landing = ((cx, 0), (R, R + cx))[side]
        target = (lax.rem(me + 1, n), lax.rem(me + n - 1, n))[side]
        return pltpu.make_async_remote_copy(
            src_ref=buf.at[pl.ds(source, R), :, rows, :],
            dst_ref=buf.at[pl.ds(landing, R), :, rows, :],
            send_sem=halo_send.at[step, side, c],
            recv_sem=halo_recv.at[step, side, c],
            device_id={"col": target},
            device_id_type=MESH,
        )

    def send_halo(buf, step, c):
        @pl.when(me < n - 1)
        def _():
            halo(buf, step, 0, c).start()

        @pl.when(me > 0)
        def _():
            halo(buf, step, 1, c).start()

    def sent_halo(buf, step, c):
        @pl.when(me < n - 1)
        def _():
            halo(buf, step, 0, c).wait_send()

        @pl.when(me > 0)
        def _():
            halo(buf, step, 1, c).wait_send()

    def take_halo(buf, step, c):
        @pl.when(me > 0)
        def _():
            halo(buf, step, 0, c).wait_recv()

        @pl.when(me < n - 1)
        def _():
            halo(buf, step, 1, c).wait_recv()

    for c in range(n_c):
        send_halo(x1, 0, c)

    def ask(k):
        target = lax.rem(me + k, n)
        return pltpu.make_async_remote_copy(
            src_ref=want_v.at[target],
            dst_ref=asked_v.at[me],
            send_sem=ask_send,
            recv_sem=ask_recv,
            device_id={"col": target},
            device_id_type=MESH,
        )

    def start_ask(k, _):
        ask(k).start()
        return 0

    lax.fori_loop(1, n, start_ask, 0)
    asked_v[me] = want_v[me]

    lane = lax.broadcasted_iota(jnp.int32, (CH, LANES), 1)
    row = lax.broadcasted_iota(jnp.int32, (CH, LANES), 0)

    def along_yz(buf):
        def plane(x, _):
            for c in range(n_c):
                tiles = [buf[R + x, j, PAD + c * CH : PAD + (c + 1) * CH, :] for j in range(n_z)]
                for j in range(n_z):
                    total = (3.0 * COEF[0]) * tiles[j]
                    for r in range(1, R + 1):
                        at = PAD + c * CH
                        pair = buf[R + x, j, at + r : at + r + CH, :] + buf[R + x, j, at - r : at - r + CH, :]
                        up = pltpu.roll(tiles[j], LANES - r, 1)
                        down = pltpu.roll(tiles[j], r, 1)
                        after = pltpu.roll(tiles[j + 1], LANES - r, 1) if j + 1 < n_z else 0.0
                        before = pltpu.roll(tiles[j - 1], r, 1) if j > 0 else 0.0
                        pair = pair + jnp.where(lane < LANES - r, up, after)
                        pair = pair + jnp.where(lane < r, before, down)
                        total = total + COEF[r] * pair
                    acc[x, j, c * CH : (c + 1) * CH, :] = total
            return 0

        lax.fori_loop(0, cx, plane, 0)

    def mask(t, c, j):
        per = CH // 4
        flags = [active_s[t, (c * per + i) * n_z + j].astype(jnp.float32) for i in range(per)]
        out = jnp.full((CH, LANES), flags[per - 1], jnp.float32)
        for i in range(per - 2, -1, -1):
            out = jnp.where(row < 4 * (i + 1), flags[i], out)
        return out

    def following(buf, x, c, j, before, flag):
        rows = slice(PAD + c * CH, PAD + (c + 1) * CH)
        total = acc[x, j, c * CH : (c + 1) * CH, :]
        for r in range(1, R + 1):
            total = total + COEF[r] * (buf[R + x + r, j, rows, :] + buf[R + x - r, j, rows, :])
        here = buf[R + x, j, rows, :]
        speed = vel_v[x, c * CH : (c + 1) * CH, j * LANES : (j + 1) * LANES]
        return here, flag * (2.0 * here - before + speed * total)

    along_yz(x1)
    load_prev.wait()
    load_vel.wait()
    for c in range(n_c):
        take_halo(x1, 0, c)
        flags = [mask(0, c, j) for j in range(n_z)]

        def plane(x, _):
            for j in range(n_z):
                before = prev_v[x, c * CH : (c + 1) * CH, j * LANES : (j + 1) * LANES]
                _, new = following(x1, x, c, j, before, flags[j])
                x2[R + x, j, PAD + c * CH : PAD + (c + 1) * CH, :] = new
            return 0

        lax.fori_loop(0, cx, plane, 0)
        send_halo(x2, 1, c)

    store_first = [
        pltpu.make_async_copy(
            x2.at[own, j, body, :], first_h.at[:, :, pl.ds(j * LANES, LANES)], out_sem.at[j]
        )
        for j in range(n_z)
    ]
    for copy in store_first:
        copy.start()

    along_yz(x2)

    pltpu.make_async_copy(
        asked_v.at[pl.ds(0, n - 1)], asked_v.at[pl.ds(0, n - 1)], ask_recv
    ).wait()
    to_scalar = pltpu.make_async_copy(asked_v, asked_s, ask_copy)
    to_scalar.start()

    load_src.wait()
    for c in range(n_c):
        take_halo(x2, 1, c)
        flags = [mask(1, c, j) for j in range(n_z)]

        def pair(p, _):
            for j in range(n_z):
                gains = []
                for i in range(2):
                    x = 2 * p + i
                    before = x1[R + x, j, PAD + c * CH : PAD + (c + 1) * CH, :]
                    here, new = following(x2, x, c, j, before, flags[j])
                    spot = (slice(c * CH, (c + 1) * CH), slice(j * LANES, (j + 1) * LANES))
                    second_v[(x,) + spot] = new
                    gains.append(
                        src_v[(0, x) + spot].astype(jnp.float32) * here
                        + src_v[(1, x) + spot].astype(jnp.float32) * new
                    )
                for h in range(CH // 8):
                    a, b = (g[h * 8 : (h + 1) * 8, :] for g in gains)
                    low = row[:8] < 4
                    even = jnp.where(low, a, pltpu.roll(b, 4, 0))
                    odd = jnp.where(low, pltpu.roll(a, 4, 0), b)
                    yb = c * (CH // 4) + 2 * h
                    for i, value in enumerate((even, odd)):
                        bricks[(yb + i) * n_z + j, pl.ds(pl.multiple_of(8 * p, 8), 8), :] = value
            return 0

        lax.fori_loop(0, cx // 2, pair, 0)

    to_scalar.wait()

    def pack(dst, at, target):
        for r in range(cap):
            dst[at + r] = bricks[asked_s[target, 0, r]]

    def give(k, target):
        return pltpu.make_async_remote_copy(
            src_ref=outgoing.at[pl.ds(k * cap, cap)],
            dst_ref=incoming.at[pl.ds(me * cap, cap)],
            send_sem=a2a_send,
            recv_sem=a2a_recv,
            device_id={"col": target},
            device_id_type=MESH,
        )

    def partner(k):
        return flipped(me, k, bits) if n == 2**bits else lax.rem(me + k, n)

    def start_give(i, _):
        k = n - 1 - i
        target = partner(k)
        pack(outgoing, k * cap, target)
        give(k, target).start()
        return 0

    lax.fori_loop(0, n - 1, start_give, 0)

    store_second = pltpu.make_async_copy(second_v, second_h, out_sem.at[n_z])
    store_second.start()
    pack(outgoing, 0, me)
    keep = pltpu.make_async_copy(
        outgoing.at[pl.ds(0, cap)], incoming.at[pl.ds(me * cap, cap)], keep_sem
    )
    keep.start()

    whole = pl.ds(cap, (n - 1) * cap)
    pltpu.make_async_copy(incoming.at[whole], incoming.at[whole], a2a_recv).wait()

    for c in range(n_c):
        sent_halo(x1, 0, c)
        sent_halo(x2, 1, c)
    pltpu.make_async_copy(
        want_v.at[pl.ds(0, n - 1)], want_v.at[pl.ds(0, n - 1)], ask_send
    ).wait()
    pltpu.make_async_copy(outgoing.at[whole], outgoing.at[whole], a2a_send).wait()
    for copy in store_first + [store_second, keep]:
        copy.wait()


def finish(
    place_s, first_h, second_h, incoming_h, img_h, first_out, second_out, image_out,
    incoming, img_v, sum_v, sem,
):
    loads = [
        pltpu.make_async_copy(incoming_h, incoming, sem.at[6]),
        pltpu.make_async_copy(img_h, img_v, sem.at[7]),
    ]
    for copy in loads:
        copy.start()
    copies = [
        pltpu.make_async_copy(first_h, first_out, sem.at[0]),
        pltpu.make_async_copy(second_h, second_out, sem.at[1]),
    ]
    for copy in copies:
        copy.start()
    per = place_s.shape[0]
    parts = 4 if per % 4 == 0 else 1
    step = per // parts
    for copy in loads:
        copy.wait()
    for q in range(parts):

        def add(i, _):
            s = q * step + i
            sum_v[s] = img_v[s] + incoming[place_s[s]]
            return 0

        lax.fori_loop(0, step, add, 0)
        span = pl.ds(q * step, step)
        copy = pltpu.make_async_copy(sum_v.at[span], image_out.at[span], sem.at[2 + q])
        copy.start()
        copies.append(copy)
    for copy in copies:
        copy.wait()


def shards(wave_prev, wave_now, velocity, source, active, plan, image_in):
    cx, ny, nz = wave_now.shape
    n = lax.axis_size("col")
    per = plan.shape[0]
    cap = (per + n - 1) // n
    n_c, n_z = ny // CH, nz // LANES

    order = jnp.arange(per, dtype=jnp.int32)
    anchor = lax.div(plan, jnp.int32(per))
    local = plan - anchor * per
    rank = jnp.sum(
        (anchor[None, :] == anchor[:, None]) & (order[None, :] < order[:, None]), axis=1, dtype=jnp.int32
    )
    place = anchor * cap + rank
    device = lax.broadcasted_iota(jnp.int32, (n, 1, LANES, per), 0)
    turn = lax.broadcasted_iota(jnp.int32, (n, 1, LANES, per), 2)
    hit = (anchor[None, None, None, :] == device) & (rank[None, None, None, :] == turn)
    want = jnp.sum(jnp.where(hit, local[None, None, None, :], 0), axis=3, dtype=jnp.int32)

    f32 = jnp.float32
    hbm = pl.BlockSpec(memory_space=pltpu.HBM)
    free = pl.BlockSpec(memory_space=pl.ANY)
    smem = pl.BlockSpec(memory_space=pltpu.SMEM)
    vmem = pl.BlockSpec(memory_space=pltpu.VMEM)
    wide = (cx + 2 * R, n_z, ny + 2 * PAD, LANES)
    dma = pltpu.SemaphoreType.DMA
    first, second, incoming = pl.pallas_call(
        functools.partial(kernel, n, cap),
        out_shape=(
            jax.ShapeDtypeStruct((cx, ny, nz), f32),
            jax.ShapeDtypeStruct((cx, ny, nz), f32),
            jax.ShapeDtypeStruct((n * cap, 32, LANES), f32),
        ),
        in_specs=[hbm] * 4 + [smem, vmem],
        out_specs=(free, free, free),
        scratch_shapes=[
            pltpu.VMEM(wide, f32),
            pltpu.VMEM(wide, f32),
            pltpu.VMEM((cx, n_z, ny, LANES), f32),
            pltpu.VMEM((cx, ny, nz), f32),
            pltpu.VMEM((cx, ny, nz), f32),
            pltpu.VMEM((2, cx, ny, nz), jnp.bfloat16),
            pltpu.VMEM((cx, ny, nz), f32),
            pltpu.VMEM((per, 32, LANES), f32),
            pltpu.VMEM((n * cap, 32, LANES), f32),
            pltpu.VMEM((n, 1, LANES), jnp.int32),
            pltpu.SMEM((n, 1, LANES), jnp.int32),
            dma((n_z + 3,)),
            dma((2, 2, n_c)),
            dma((2, 2, n_c)),
            dma(()),
            dma(()),
            dma(()),
            dma(()),
            dma(()),
            dma(()),
            dma((n_z + 1,)),
        ],
        compiler_params=pltpu.CompilerParams(
            collective_id=0, has_side_effects=True, vmem_limit_bytes=60 * 2**20
        ),
    )(
        wave_prev, wave_now, velocity, source, active, want
    )
    first, second, image = pl.pallas_call(
        finish,
        out_shape=(
            jax.ShapeDtypeStruct((cx, ny, nz), f32),
            jax.ShapeDtypeStruct((cx, ny, nz), f32),
            jax.ShapeDtypeStruct((per, 32, LANES), f32),
        ),
        in_specs=[smem, free, free, free, free],
        out_specs=(hbm, hbm, hbm),
        scratch_shapes=[
            pltpu.VMEM((n * cap, 32, LANES), f32),
            pltpu.VMEM((per, 32, LANES), f32),
            pltpu.VMEM((per, 32, LANES), f32),
            dma((8,)),
        ],
        compiler_params=pltpu.CompilerParams(vmem_limit_bytes=60 * 2**20),
    )(place, first, second, incoming, image_in.reshape(per, 32, LANES))
    return first, second, image.reshape(image_in.shape)


def solution(mesh):
    lead = ("shot", "col")
    in_specs = (
        P(lead, None, None),
        P(lead, None, None),
        P(lead, None, None),
        P(None, lead, None, None),
        P(None, lead),
        P(lead),
        P(lead, None, None, None),
    )
    out_specs = (P(lead, None, None), P(lead, None, None), P(lead, None, None, None))
    return jax.shard_map(shards, mesh=mesh, in_specs=in_specs, out_specs=out_specs, check_vma=False)
```

```python
import functools

import jax
import jax.numpy as jnp
from jax import lax
from jax.experimental import pallas as pl
from jax.experimental.pallas import tpu as pltpu
from jax.sharding import PartitionSpec as P

COEF = (-205.0 / 72.0, 8.0 / 5.0, -1.0 / 5.0, 8.0 / 315.0, -1.0 / 560.0)
MESH = pl.DeviceIdType.MESH
R = 4
PAD = 8
CH = 16
LANES = 128


def flipped(me, k, bits):
    out = me
    for b in range(bits):
        out = out + ((k // 2**b) % 2) * (2**b) * (1 - 2 * ((me // 2**b) % 2))
    return out


def kernel(
    n, cap, prev_h, now_h, vel_h, src_h, active_h, plan_h,
    first_h, second_h, incoming, place_v,
    x1, x2, acc, prev_v, vel_v, src_v, second_v, bricks, outgoing, active_s, plan_s, want_2d, want_v, asked_v, asked_s,
    in_sem, halo_send, halo_recv, ask_send, ask_recv, ask_copy, a2a_send, a2a_recv, keep_sem, out_sem,
):
    me = lax.axis_index("col")
    cx, ny, nz = prev_h.shape
    n_c, n_z = ny // CH, nz // LANES
    bits = (n - 1).bit_length()

    def zero_rows(x, _):
        for j in range(n_z):
            for buf in (x1, x2):
                buf[R + x, j, 0:PAD, :] = jnp.zeros((PAD, LANES), jnp.float32)
                buf[R + x, j, PAD + ny : PAD + ny + PAD, :] = jnp.zeros((PAD, LANES), jnp.float32)
        return 0

    own = pl.ds(R, cx)
    body = pl.ds(PAD, ny)
    load_now = [
        pltpu.make_async_copy(
            now_h.at[:, :, pl.ds(j * LANES, LANES)], x1.at[own, j, body, :], in_sem.at[j]
        )
        for j in range(n_z)
    ]
    for copy in load_now:
        copy.start()
    load_plan = pltpu.make_async_copy(plan_h, plan_s, in_sem.at[n_z + 3])
    load_active = pltpu.make_async_copy(active_h, active_s, in_sem.at[n_z + 4])
    load_plan.start()
    load_active.start()
    load_prev = pltpu.make_async_copy(prev_h, prev_v, in_sem.at[n_z])
    load_vel = pltpu.make_async_copy(vel_h, vel_v, in_sem.at[n_z + 1])
    load_src = pltpu.make_async_copy(src_h, src_v, in_sem.at[n_z + 2])
    for copy in (load_prev, load_vel, load_src):
        copy.start()

    barrier = pltpu.get_barrier_semaphore()

    def greet(k, _):
        pl.semaphore_signal(
            barrier, inc=1, device_id={"col": lax.rem(me + k, n)}, device_id_type=MESH
        )
        return 0

    lax.fori_loop(1, n, greet, 0)

    lax.fori_loop(0, cx, zero_rows, 0)

    def zero_halo(start):
        def plane(x, _):
            for buf in (x1, x2):
                for j in range(n_z):
                    buf[start + x, j, PAD : PAD + ny, :] = jnp.zeros((ny, LANES), jnp.float32)
            return 0

        lax.fori_loop(0, R, plane, 0)

    @pl.when(me == 0)
    def _():
        zero_halo(0)

    @pl.when(me == n - 1)
    def _():
        zero_halo(R + cx)

    for copy in load_now:
        copy.wait()
    pl.semaphore_wait(barrier, n - 1)

    def halo(buf, step, side, c):
        rows = pl.ds(PAD + c * CH, CH)
        source, landing = ((cx, 0), (R, R + cx))[side]
        target = (lax.rem(me + 1, n), lax.rem(me + n - 1, n))[side]
        return pltpu.make_async_remote_copy(
            src_ref=buf.at[pl.ds(source, R), :, rows, :],
            dst_ref=buf.at[pl.ds(landing, R), :, rows, :],
            send_sem=halo_send.at[step, side, c],
            recv_sem=halo_recv.at[step, side, c],
            device_id={"col": target},
            device_id_type=MESH,
        )

    def send_halo(buf, step, c):
        @pl.when(me < n - 1)
        def _():
            halo(buf, step, 0, c).start()

        @pl.when(me > 0)
        def _():
            halo(buf, step, 1, c).start()

    def sent_halo(buf, step, c):
        @pl.when(me < n - 1)
        def _():
            halo(buf, step, 0, c).wait_send()

        @pl.when(me > 0)
        def _():
            halo(buf, step, 1, c).wait_send()

    def take_halo(buf, step, c):
        @pl.when(me > 0)
        def _():
            halo(buf, step, 0, c).wait_recv()

        @pl.when(me < n - 1)
        def _():
            halo(buf, step, 1, c).wait_recv()

    for c in range(n_c):
        send_halo(x1, 0, c)

    load_plan.wait()
    load_active.wait()
    per = plan_s.shape[0]
    slot = lax.broadcasted_iota(jnp.int32, (8, LANES), 1)
    zero = jnp.zeros((8, LANES), jnp.int32)

    def spread(s, carry):
        anchor, local = carry
        device = lax.div(plan_s[s], per)
        here = slot == s
        return jnp.where(here, device, anchor), jnp.where(here, plan_s[s] - device * per, local)

    anchor, local = lax.fori_loop(0, per, spread, (zero - 1, zero), unroll=8)

    def count(s, rank):
        device = lax.div(plan_s[s], per)
        return rank + jnp.where((slot > s) & (anchor == device), 1, 0)

    rank = lax.fori_loop(0, per, count, zero, unroll=8)
    place_v[...] = (anchor * cap + rank)[:1]

    def table(i, _):
        device = lax.broadcasted_iota(jnp.int32, (8, LANES), 0) + 8 * i
        rows = zero
        for r in range(cap):
            hit = (anchor == device) & (rank == r)
            pick = jnp.sum(jnp.where(hit, local, 0), axis=1, keepdims=True)
            rows = jnp.where(slot == r, pick, rows)
        want_2d[pl.ds(pl.multiple_of(8 * i, 8), 8), :] = rows
        return 0

    lax.fori_loop(0, (n + 7) // 8, table, 0)

    def lay(k, _):
        want_v[k] = want_2d[pl.ds(k, 1), :]
        return 0

    lax.fori_loop(0, n, lay, 0)

    def ask(k):
        target = lax.rem(me + k, n)
        return pltpu.make_async_remote_copy(
            src_ref=want_v.at[target],
            dst_ref=asked_v.at[me],
            send_sem=ask_send,
            recv_sem=ask_recv,
            device_id={"col": target},
            device_id_type=MESH,
        )

    def start_ask(k, _):
        ask(k).start()
        return 0

    lax.fori_loop(1, n, start_ask, 0)
    asked_v[me] = want_v[me]

    lane = lax.broadcasted_iota(jnp.int32, (CH, LANES), 1)
    row = lax.broadcasted_iota(jnp.int32, (CH, LANES), 0)

    def along_yz(buf):
        def plane(x, _):
            for c in range(n_c):
                tiles = [buf[R + x, j, PAD + c * CH : PAD + (c + 1) * CH, :] for j in range(n_z)]
                for j in range(n_z):
                    total = (3.0 * COEF[0]) * tiles[j]
                    for r in range(1, R + 1):
                        at = PAD + c * CH
                        pair = buf[R + x, j, at + r : at + r + CH, :] + buf[R + x, j, at - r : at - r + CH, :]
                        up = pltpu.roll(tiles[j], LANES - r, 1)
                        down = pltpu.roll(tiles[j], r, 1)
                        after = pltpu.roll(tiles[j + 1], LANES - r, 1) if j + 1 < n_z else 0.0
                        before = pltpu.roll(tiles[j - 1], r, 1) if j > 0 else 0.0
                        pair = pair + jnp.where(lane < LANES - r, up, after)
                        pair = pair + jnp.where(lane < r, before, down)
                        total = total + COEF[r] * pair
                    acc[x, j, c * CH : (c + 1) * CH, :] = total
            return 0

        lax.fori_loop(0, cx, plane, 0)

    def mask(t, c, j):
        per = CH // 4
        flags = [active_s[t, (c * per + i) * n_z + j].astype(jnp.float32) for i in range(per)]
        out = jnp.full((CH, LANES), flags[per - 1], jnp.float32)
        for i in range(per - 2, -1, -1):
            out = jnp.where(row < 4 * (i + 1), flags[i], out)
        return out

    def following(buf, x, c, j, before, flag):
        rows = slice(PAD + c * CH, PAD + (c + 1) * CH)
        total = acc[x, j, c * CH : (c + 1) * CH, :]
        for r in range(1, R + 1):
            total = total + COEF[r] * (buf[R + x + r, j, rows, :] + buf[R + x - r, j, rows, :])
        here = buf[R + x, j, rows, :]
        speed = vel_v[x, c * CH : (c + 1) * CH, j * LANES : (j + 1) * LANES]
        return here, flag * (2.0 * here - before + speed * total)

    along_yz(x1)
    load_prev.wait()
    load_vel.wait()
    for c in range(n_c):
        take_halo(x1, 0, c)
        flags = [mask(0, c, j) for j in range(n_z)]

        def plane(x, _):
            for j in range(n_z):
                before = prev_v[x, c * CH : (c + 1) * CH, j * LANES : (j + 1) * LANES]
                _, new = following(x1, x, c, j, before, flags[j])
                x2[R + x, j, PAD + c * CH : PAD + (c + 1) * CH, :] = new
            return 0

        lax.fori_loop(0, cx, plane, 0)
        send_halo(x2, 1, c)

    store_first = [
        pltpu.make_async_copy(
            x2.at[own, j, body, :], first_h.at[:, :, pl.ds(j * LANES, LANES)], out_sem.at[j]
        )
        for j in range(n_z)
    ]
    for copy in store_first:
        copy.start()

    along_yz(x2)

    pltpu.make_async_copy(
        asked_v.at[pl.ds(0, n - 1)], asked_v.at[pl.ds(0, n - 1)], ask_recv
    ).wait()
    to_scalar = pltpu.make_async_copy(asked_v, asked_s, ask_copy)
    to_scalar.start()

    load_src.wait()
    for c in range(n_c):
        take_halo(x2, 1, c)
        flags = [mask(1, c, j) for j in range(n_z)]

        def pair(p, _):
            for j in range(n_z):
                gains = []
                for i in range(2):
                    x = 2 * p + i
                    before = x1[R + x, j, PAD + c * CH : PAD + (c + 1) * CH, :]
                    here, new = following(x2, x, c, j, before, flags[j])
                    spot = (slice(c * CH, (c + 1) * CH), slice(j * LANES, (j + 1) * LANES))
                    second_v[(x,) + spot] = new
                    gains.append(
                        src_v[(0, x) + spot].astype(jnp.float32) * here
                        + src_v[(1, x) + spot].astype(jnp.float32) * new
                    )
                for h in range(CH // 8):
                    a, b = (g[h * 8 : (h + 1) * 8, :] for g in gains)
                    low = row[:8] < 4
                    even = jnp.where(low, a, pltpu.roll(b, 4, 0))
                    odd = jnp.where(low, pltpu.roll(a, 4, 0), b)
                    yb = c * (CH // 4) + 2 * h
                    for i, value in enumerate((even, odd)):
                        bricks[(yb + i) * n_z + j, pl.ds(pl.multiple_of(8 * p, 8), 8), :] = value
            return 0

        lax.fori_loop(0, cx // 2, pair, 0)

    to_scalar.wait()

    def pack(dst, at, target):
        for r in range(cap):
            dst[at + r] = bricks[asked_s[target, 0, r]]

    def give(k, target):
        return pltpu.make_async_remote_copy(
            src_ref=outgoing.at[pl.ds(k * cap, cap)],
            dst_ref=incoming.at[pl.ds(me * cap, cap)],
            send_sem=a2a_send,
            recv_sem=a2a_recv,
            device_id={"col": target},
            device_id_type=MESH,
        )

    def partner(k):
        return flipped(me, k, bits) if n == 2**bits else lax.rem(me + k, n)

    def start_give(i, _):
        k = n - 1 - i
        target = partner(k)
        pack(outgoing, k * cap, target)
        give(k, target).start()
        return 0

    lax.fori_loop(0, n - 1, start_give, 0)

    store_second = pltpu.make_async_copy(second_v, second_h, out_sem.at[n_z])
    store_second.start()
    pack(outgoing, 0, me)
    keep = pltpu.make_async_copy(
        outgoing.at[pl.ds(0, cap)], incoming.at[pl.ds(me * cap, cap)], keep_sem
    )
    keep.start()

    whole = pl.ds(cap, (n - 1) * cap)
    pltpu.make_async_copy(incoming.at[whole], incoming.at[whole], a2a_recv).wait()

    for c in range(n_c):
        sent_halo(x1, 0, c)
        sent_halo(x2, 1, c)
    pltpu.make_async_copy(
        want_v.at[pl.ds(0, n - 1)], want_v.at[pl.ds(0, n - 1)], ask_send
    ).wait()
    pltpu.make_async_copy(outgoing.at[whole], outgoing.at[whole], a2a_send).wait()
    for copy in store_first + [store_second, keep]:
        copy.wait()


def finish(
    place_s, first_h, second_h, incoming_h, img_h, first_out, second_out, image_out,
    first_v, second_v, incoming, img_v, sum_v, sem,
):
    waves = [
        pltpu.make_async_copy(first_h, first_v, sem.at[8]),
        pltpu.make_async_copy(second_h, second_v, sem.at[9]),
    ]
    loads = [
        pltpu.make_async_copy(incoming_h, incoming, sem.at[6]),
        pltpu.make_async_copy(img_h, img_v, sem.at[7]),
    ]
    for copy in waves + loads:
        copy.start()
    copies = [
        pltpu.make_async_copy(first_v, first_out, sem.at[0]),
        pltpu.make_async_copy(second_v, second_out, sem.at[1]),
    ]
    for load, copy in zip(waves, copies):
        load.wait()
        copy.start()
    per = img_v.shape[0]
    parts = 4 if per % 4 == 0 else 1
    step = per // parts
    for copy in loads:
        copy.wait()
    for q in range(parts):

        def add(i, _):
            s = q * step + i
            sum_v[s] = img_v[s] + incoming[place_s[0, s]]
            return 0

        lax.fori_loop(0, step, add, 0)
        span = pl.ds(q * step, step)
        copy = pltpu.make_async_copy(sum_v.at[span], image_out.at[span], sem.at[2 + q])
        copy.start()
        copies.append(copy)
    for copy in copies:
        copy.wait()


def shards(wave_prev, wave_now, velocity, source, active, plan, image_in):
    cx, ny, nz = wave_now.shape
    n = lax.axis_size("col")
    per = plan.shape[0]
    cap = (per + n - 1) // n
    n_c, n_z = ny // CH, nz // LANES

    f32 = jnp.float32
    hbm = pl.BlockSpec(memory_space=pltpu.HBM)
    free = pl.BlockSpec(memory_space=pl.ANY)
    smem = pl.BlockSpec(memory_space=pltpu.SMEM)
    vmem = pl.BlockSpec(memory_space=pltpu.VMEM)
    assert per <= LANES
    wide = (cx + 2 * R, n_z, ny + 2 * PAD, LANES)
    dma = pltpu.SemaphoreType.DMA
    first, second, incoming, place = pl.pallas_call(
        functools.partial(kernel, n, cap),
        out_shape=(
            jax.ShapeDtypeStruct((cx, ny, nz), f32),
            jax.ShapeDtypeStruct((cx, ny, nz), f32),
            jax.ShapeDtypeStruct((n * cap, 32, LANES), f32),
            jax.ShapeDtypeStruct((1, LANES), jnp.int32),
        ),
        in_specs=[hbm] * 6,
        out_specs=(free, free, free, vmem),
        scratch_shapes=[
            pltpu.VMEM(wide, f32),
            pltpu.VMEM(wide, f32),
            pltpu.VMEM((cx, n_z, ny, LANES), f32),
            pltpu.VMEM((cx, ny, nz), f32),
            pltpu.VMEM((cx, ny, nz), f32),
            pltpu.VMEM((2, cx, ny, nz), jnp.bfloat16),
            pltpu.VMEM((cx, ny, nz), f32),
            pltpu.VMEM((per, 32, LANES), f32),
            pltpu.VMEM((n * cap, 32, LANES), f32),
            pltpu.SMEM(active.shape, jnp.int32),
            pltpu.SMEM((per,), jnp.int32),
            pltpu.VMEM(((n + 7) // 8 * 8, LANES), jnp.int32),
            pltpu.VMEM((n, 1, LANES), jnp.int32),
            pltpu.VMEM((n, 1, LANES), jnp.int32),
            pltpu.SMEM((n, 1, LANES), jnp.int32),
            dma((n_z + 5,)),
            dma((2, 2, n_c)),
            dma((2, 2, n_c)),
            dma(()),
            dma(()),
            dma(()),
            dma(()),
            dma(()),
            dma(()),
            dma((n_z + 1,)),
        ],
        compiler_params=pltpu.CompilerParams(
            collective_id=0, has_side_effects=True, vmem_limit_bytes=60 * 2**20
        ),
    )(
        wave_prev, wave_now, velocity, source, active, plan
    )
    first, second, image = pl.pallas_call(
        finish,
        out_shape=(
            jax.ShapeDtypeStruct((cx, ny, nz), f32),
            jax.ShapeDtypeStruct((cx, ny, nz), f32),
            jax.ShapeDtypeStruct((per, 32, LANES), f32),
        ),
        in_specs=[smem, free, free, free, free],
        out_specs=(hbm, hbm, hbm),
        scratch_shapes=[
            pltpu.VMEM((cx, ny, nz), f32),
            pltpu.VMEM((cx, ny, nz), f32),
            pltpu.VMEM((n * cap, 32, LANES), f32),
            pltpu.VMEM((per, 32, LANES), f32),
            pltpu.VMEM((per, 32, LANES), f32),
            dma((10,)),
        ],
        compiler_params=pltpu.CompilerParams(vmem_limit_bytes=60 * 2**20),
    )(place, first, second, incoming, image_in.reshape(per, 32, LANES))
    return first, second, image.reshape(image_in.shape)


def solution(mesh):
    lead = ("shot", "col")
    in_specs = (
        P(lead, None, None),
        P(lead, None, None),
        P(lead, None, None),
        P(None, lead, None, None),
        P(None, lead),
        P(lead),
        P(lead, None, None, None),
    )
    out_specs = (P(lead, None, None), P(lead, None, None), P(lead, None, None, None))
    return jax.shard_map(shards, mesh=mesh, in_specs=in_specs, out_specs=out_specs, check_vma=False)
```

```python
import functools

import jax
import jax.numpy as jnp
from jax import lax
from jax.experimental import pallas as pl
from jax.experimental.pallas import tpu as pltpu
from jax.sharding import PartitionSpec as P

COEF = (-205.0 / 72.0, 8.0 / 5.0, -1.0 / 5.0, 8.0 / 315.0, -1.0 / 560.0)
MESH = pl.DeviceIdType.MESH
R = 4
PAD = 8
CH = 16
LANES = 128


def flipped(me, k, bits):
    out = me
    for b in range(bits):
        out = out + ((k // 2**b) % 2) * (2**b) * (1 - 2 * ((me // 2**b) % 2))
    return out


def kernel(
    n, cap, prev_h, now_h, vel_h, src_h, active_h, plan_h,
    first_h, second_h, incoming, place_v,
    x1, x2, acc, prev_v, vel_v, src_v, second_v, bricks, outgoing, active_s, plan_s, want_2d, want_v, asked_v, asked_s,
    in_sem, halo_send, halo_recv, ask_send, ask_recv, ask_copy, a2a_send, a2a_recv, keep_sem, out_sem,
):
    me = lax.axis_index("col")
    cx, ny, nz = prev_h.shape
    n_c, n_z = ny // CH, nz // LANES
    bits = (n - 1).bit_length()

    def zero_rows(x, _):
        for j in range(n_z):
            for buf in (x1, x2):
                buf[R + x, j, 0:PAD, :] = jnp.zeros((PAD, LANES), jnp.float32)
                buf[R + x, j, PAD + ny : PAD + ny + PAD, :] = jnp.zeros((PAD, LANES), jnp.float32)
        return 0

    own = pl.ds(R, cx)
    body = pl.ds(PAD, ny)
    load_now = [
        pltpu.make_async_copy(
            now_h.at[:, :, pl.ds(j * LANES, LANES)], x1.at[own, j, body, :], in_sem.at[j]
        )
        for j in range(n_z)
    ]
    for copy in load_now:
        copy.start()
    load_plan = pltpu.make_async_copy(plan_h, plan_s, in_sem.at[n_z + 3])
    load_active = pltpu.make_async_copy(active_h, active_s, in_sem.at[n_z + 4])
    load_plan.start()
    load_active.start()
    load_prev = pltpu.make_async_copy(prev_h, prev_v, in_sem.at[n_z])
    load_vel = pltpu.make_async_copy(vel_h, vel_v, in_sem.at[n_z + 1])
    load_src = pltpu.make_async_copy(src_h, src_v, in_sem.at[n_z + 2])
    for copy in (load_prev, load_vel, load_src):
        copy.start()

    barrier = pltpu.get_barrier_semaphore()

    def greet(k, _):
        pl.semaphore_signal(
            barrier, inc=1, device_id={"col": lax.rem(me + k, n)}, device_id_type=MESH
        )
        return 0

    lax.fori_loop(1, n, greet, 0)

    lax.fori_loop(0, cx, zero_rows, 0)

    def zero_halo(start):
        def plane(x, _):
            for buf in (x1, x2):
                for j in range(n_z):
                    buf[start + x, j, PAD : PAD + ny, :] = jnp.zeros((ny, LANES), jnp.float32)
            return 0

        lax.fori_loop(0, R, plane, 0)

    @pl.when(me == 0)
    def _():
        zero_halo(0)

    @pl.when(me == n - 1)
    def _():
        zero_halo(R + cx)

    for copy in load_now:
        copy.wait()
    pl.semaphore_wait(barrier, n - 1)

    def halo(buf, step, side, c):
        rows = pl.ds(PAD + c * CH, CH)
        source, landing = ((cx, 0), (R, R + cx))[side]
        target = (lax.rem(me + 1, n), lax.rem(me + n - 1, n))[side]
        return pltpu.make_async_remote_copy(
            src_ref=buf.at[pl.ds(source, R), :, rows, :],
            dst_ref=buf.at[pl.ds(landing, R), :, rows, :],
            send_sem=halo_send.at[step, side, c],
            recv_sem=halo_recv.at[step, side, c],
            device_id={"col": target},
            device_id_type=MESH,
        )

    def send_halo(buf, step, c):
        @pl.when(me < n - 1)
        def _():
            halo(buf, step, 0, c).start()

        @pl.when(me > 0)
        def _():
            halo(buf, step, 1, c).start()

    def sent_halo(buf, step, c):
        @pl.when(me < n - 1)
        def _():
            halo(buf, step, 0, c).wait_send()

        @pl.when(me > 0)
        def _():
            halo(buf, step, 1, c).wait_send()

    def take_halo(buf, step, c):
        @pl.when(me > 0)
        def _():
            halo(buf, step, 0, c).wait_recv()

        @pl.when(me < n - 1)
        def _():
            halo(buf, step, 1, c).wait_recv()

    for c in range(n_c):
        send_halo(x1, 0, c)

    load_plan.wait()
    load_active.wait()
    per = plan_s.shape[0]
    slot = lax.broadcasted_iota(jnp.int32, (8, LANES), 1)
    zero = jnp.zeros((8, LANES), jnp.int32)

    def spread(s, carry):
        anchor, local = carry
        device = lax.div(plan_s[s], per)
        here = slot == s
        return jnp.where(here, device, anchor), jnp.where(here, plan_s[s] - device * per, local)

    anchor, local = lax.fori_loop(0, per, spread, (zero - 1, zero), unroll=8)

    def count(s, rank):
        device = lax.div(plan_s[s], per)
        return rank + jnp.where((slot > s) & (anchor == device), 1, 0)

    rank = lax.fori_loop(0, per, count, zero, unroll=8)
    place_v[...] = (anchor * cap + rank)[:1]

    def table(i, _):
        device = lax.broadcasted_iota(jnp.int32, (8, LANES), 0) + 8 * i
        rows = zero
        for r in range(cap):
            hit = (anchor == device) & (rank == r)
            pick = jnp.sum(jnp.where(hit, local, 0), axis=1, keepdims=True)
            rows = jnp.where(slot == r, pick, rows)
        want_2d[pl.ds(pl.multiple_of(8 * i, 8), 8), :] = rows
        return 0

    lax.fori_loop(0, (n + 7) // 8, table, 0)

    def lay(k, _):
        want_v[k] = want_2d[pl.ds(k, 1), :]
        return 0

    lax.fori_loop(0, n, lay, 0)

    def ask(k):
        target = lax.rem(me + k, n)
        return pltpu.make_async_remote_copy(
            src_ref=want_v.at[target],
            dst_ref=asked_v.at[me],
            send_sem=ask_send,
            recv_sem=ask_recv,
            device_id={"col": target},
            device_id_type=MESH,
        )

    def start_ask(k, _):
        ask(k).start()
        return 0

    lax.fori_loop(1, n, start_ask, 0)
    asked_v[me] = want_v[me]

    lane = lax.broadcasted_iota(jnp.int32, (CH, LANES), 1)
    row = lax.broadcasted_iota(jnp.int32, (CH, LANES), 0)

    def along_yz(buf):
        def plane(x, _):
            for c in range(n_c):
                tiles = [buf[R + x, j, PAD + c * CH : PAD + (c + 1) * CH, :] for j in range(n_z)]
                for j in range(n_z):
                    total = (3.0 * COEF[0]) * tiles[j]
                    for r in range(1, R + 1):
                        at = PAD + c * CH
                        pair = buf[R + x, j, at + r : at + r + CH, :] + buf[R + x, j, at - r : at - r + CH, :]
                        up = pltpu.roll(tiles[j], LANES - r, 1)
                        down = pltpu.roll(tiles[j], r, 1)
                        after = pltpu.roll(tiles[j + 1], LANES - r, 1) if j + 1 < n_z else 0.0
                        before = pltpu.roll(tiles[j - 1], r, 1) if j > 0 else 0.0
                        pair = pair + jnp.where(lane < LANES - r, up, after)
                        pair = pair + jnp.where(lane < r, before, down)
                        total = total + COEF[r] * pair
                    acc[x, j, c * CH : (c + 1) * CH, :] = total
            return 0

        lax.fori_loop(0, cx, plane, 0)

    def mask(t, c, j):
        per = CH // 4
        flags = [active_s[t, (c * per + i) * n_z + j].astype(jnp.float32) for i in range(per)]
        out = jnp.full((CH, LANES), flags[per - 1], jnp.float32)
        for i in range(per - 2, -1, -1):
            out = jnp.where(row < 4 * (i + 1), flags[i], out)
        return out

    def following(buf, x, c, j, before, flag):
        rows = slice(PAD + c * CH, PAD + (c + 1) * CH)
        total = acc[x, j, c * CH : (c + 1) * CH, :]
        for r in range(1, R + 1):
            total = total + COEF[r] * (buf[R + x + r, j, rows, :] + buf[R + x - r, j, rows, :])
        here = buf[R + x, j, rows, :]
        speed = vel_v[x, c * CH : (c + 1) * CH, j * LANES : (j + 1) * LANES]
        return here, flag * (2.0 * here - before + speed * total)

    even = lax.rem(me, 2) == 0

    def take_near(buf, step, c):
        @pl.when(jnp.logical_not(even))
        def _():
            halo(buf, step, 0, c).wait_recv()

        @pl.when(even & (me < n - 1))
        def _():
            halo(buf, step, 1, c).wait_recv()

    def take_other(buf, step, c):
        @pl.when(even & (me > 0))
        def _():
            halo(buf, step, 0, c).wait_recv()

        @pl.when(jnp.logical_not(even) & (me < n - 1))
        def _():
            halo(buf, step, 1, c).wait_recv()

    along_yz(x1)
    load_prev.wait()
    load_vel.wait()
    for c in range(n_c):
        take_halo(x1, 0, c)
        flags = [mask(0, c, j) for j in range(n_z)]

        def plane(x, _):
            for j in range(n_z):
                before = prev_v[x, c * CH : (c + 1) * CH, j * LANES : (j + 1) * LANES]
                _, new = following(x1, x, c, j, before, flags[j])
                x2[R + x, j, PAD + c * CH : PAD + (c + 1) * CH, :] = new
            return 0

        lax.fori_loop(0, cx, plane, 0)
        send_halo(x2, 1, c)

    store_first = [
        pltpu.make_async_copy(
            x2.at[own, j, body, :], first_h.at[:, :, pl.ds(j * LANES, LANES)], out_sem.at[j]
        )
        for j in range(n_z)
    ]
    for copy in store_first:
        copy.start()

    along_yz(x2)

    pltpu.make_async_copy(
        asked_v.at[pl.ds(0, n - 1)], asked_v.at[pl.ds(0, n - 1)], ask_recv
    ).wait()
    to_scalar = pltpu.make_async_copy(asked_v, asked_s, ask_copy)
    to_scalar.start()

    load_src.wait()
    half = cx // 2
    base_near = half * (1 - lax.rem(me, 2))

    def second_half(phase, take, base):
        for c in range(n_c):
            take(x2, 1, c)
            flags = [mask(1, c, j) for j in range(n_z)]

            def pair(p, _):
                for j in range(n_z):
                    gains = []
                    for i in range(2):
                        x = base + 2 * p + i
                        before = x1[R + x, j, PAD + c * CH : PAD + (c + 1) * CH, :]
                        here, new = following(x2, x, c, j, before, flags[j])
                        spot = (slice(c * CH, (c + 1) * CH), slice(j * LANES, (j + 1) * LANES))
                        second_v[(x,) + spot] = new
                        gains.append(
                            src_v[(0, x) + spot].astype(jnp.float32) * here
                            + src_v[(1, x) + spot].astype(jnp.float32) * new
                        )
                    for h in range(CH // 8):
                        a, b = (g[h * 8 : (h + 1) * 8, :] for g in gains)
                        low = row[:8] < 4
                        first = jnp.where(low, a, pltpu.roll(b, 4, 0))
                        other = jnp.where(low, pltpu.roll(a, 4, 0), b)
                        yb = c * (CH // 4) + 2 * h
                        for i, value in enumerate((first, other)):
                            at = (yb + i) * n_z + j
                            bricks[phase, at, pl.ds(pl.multiple_of(8 * p, 8), 8), :] = value
                return 0

            lax.fori_loop(0, half // 2, pair, 0)

    def pack(phase, k, target):
        for r in range(cap):
            outgoing[phase, k * cap + r] = bricks[phase, asked_s[target, 0, r]]

    def landing(base):
        rows = pl.ds(pl.multiple_of(base * 4, 16), half * 4)
        return incoming.at[pl.ds(me * cap, cap), rows, :]

    bases = (base_near, half - base_near)

    def give(phase, k):
        target = flipped(me, k, bits) if n == 2**bits else lax.rem(me + k, n)
        pack(phase, k, target)
        pltpu.make_async_remote_copy(
            src_ref=outgoing.at[phase, pl.ds(k * cap, cap)],
            dst_ref=landing(bases[phase]),
            send_sem=a2a_send,
            recv_sem=a2a_recv,
            device_id={"col": target},
            device_id_type=MESH,
        ).start()

    def give_group(phase, start, top, shift):
        def one(i, _):
            give(phase, top + (i // 2) * 4 + shift + i % 2)
            return 0

        lax.fori_loop(start, n // 4, one, 0)

    def give_all(phase):
        def one(i, _):
            give(phase, i)
            return 0

        lax.fori_loop(1, n, one, 0)

    grouped = n == 2**bits and n >= 8
    second_half(0, take_near, bases[0])
    to_scalar.wait()
    if grouped:
        give_group(0, 0, n // 2, 0)
        give_group(0, 0, n // 2, 2)
        give_group(0, 1, 0, 0)
    else:
        give_all(0)
    second_half(1, take_other, bases[1])
    if grouped:
        give_group(1, 0, n // 2, 0)
        give_group(1, 0, n // 2, 2)
        give_group(0, 0, 0, 2)
        give_group(1, 0, 0, 2)
        give_group(1, 1, 0, 0)
    else:
        give_all(1)

    store_second = pltpu.make_async_copy(second_v, second_h, out_sem.at[n_z])
    store_second.start()
    keeps = []
    for phase in range(2):
        pack(phase, 0, me)
        keep = pltpu.make_async_copy(
            outgoing.at[phase, pl.ds(0, cap)], landing(bases[phase]), keep_sem.at[phase]
        )
        keep.start()
        keeps.append(keep)

    whole = pl.ds(cap, (n - 1) * cap)
    pltpu.make_async_copy(incoming.at[whole], incoming.at[whole], a2a_recv).wait()

    for c in range(n_c):
        sent_halo(x1, 0, c)
        sent_halo(x2, 1, c)
    pltpu.make_async_copy(
        want_v.at[pl.ds(0, n - 1)], want_v.at[pl.ds(0, n - 1)], ask_send
    ).wait()
    pltpu.make_async_copy(outgoing.at[:, whole], outgoing.at[:, whole], a2a_send).wait()
    for copy in store_first + [store_second] + keeps:
        copy.wait()


def finish(
    place_s, first_h, second_h, incoming_h, img_h, first_out, second_out, image_out,
    first_v, second_v, incoming, img_v, sum_v, sem,
):
    waves = [
        pltpu.make_async_copy(first_h, first_v, sem.at[8]),
        pltpu.make_async_copy(second_h, second_v, sem.at[9]),
    ]
    loads = [
        pltpu.make_async_copy(incoming_h, incoming, sem.at[6]),
        pltpu.make_async_copy(img_h, img_v, sem.at[7]),
    ]
    for copy in waves + loads:
        copy.start()
    copies = [
        pltpu.make_async_copy(first_v, first_out, sem.at[0]),
        pltpu.make_async_copy(second_v, second_out, sem.at[1]),
    ]
    for load, copy in zip(waves, copies):
        load.wait()
        copy.start()
    per = img_v.shape[0]
    parts = 4 if per % 4 == 0 else 1
    step = per // parts
    for copy in loads:
        copy.wait()
    for q in range(parts):

        def add(i, _):
            s = q * step + i
            sum_v[s] = img_v[s] + incoming[place_s[0, s]]
            return 0

        lax.fori_loop(0, step, add, 0)
        span = pl.ds(q * step, step)
        copy = pltpu.make_async_copy(sum_v.at[span], image_out.at[span], sem.at[2 + q])
        copy.start()
        copies.append(copy)
    for copy in copies:
        copy.wait()


def shards(wave_prev, wave_now, velocity, source, active, plan, image_in):
    cx, ny, nz = wave_now.shape
    n = lax.axis_size("col")
    per = plan.shape[0]
    cap = (per + n - 1) // n
    n_c, n_z = ny // CH, nz // LANES

    f32 = jnp.float32
    hbm = pl.BlockSpec(memory_space=pltpu.HBM)
    free = pl.BlockSpec(memory_space=pl.ANY)
    smem = pl.BlockSpec(memory_space=pltpu.SMEM)
    vmem = pl.BlockSpec(memory_space=pltpu.VMEM)
    assert per <= LANES
    wide = (cx + 2 * R, n_z, ny + 2 * PAD, LANES)
    dma = pltpu.SemaphoreType.DMA
    first, second, incoming, place = pl.pallas_call(
        functools.partial(kernel, n, cap),
        out_shape=(
            jax.ShapeDtypeStruct((cx, ny, nz), f32),
            jax.ShapeDtypeStruct((cx, ny, nz), f32),
            jax.ShapeDtypeStruct((n * cap, 32, LANES), f32),
            jax.ShapeDtypeStruct((1, LANES), jnp.int32),
        ),
        in_specs=[hbm] * 6,
        out_specs=(free, free, free, vmem),
        scratch_shapes=[
            pltpu.VMEM(wide, f32),
            pltpu.VMEM(wide, f32),
            pltpu.VMEM((cx, n_z, ny, LANES), f32),
            pltpu.VMEM((cx, ny, nz), f32),
            pltpu.VMEM((cx, ny, nz), f32),
            pltpu.VMEM((2, cx, ny, nz), jnp.bfloat16),
            pltpu.VMEM((cx, ny, nz), f32),
            pltpu.VMEM((2, per, 16, LANES), f32),
            pltpu.VMEM((2, n * cap, 16, LANES), f32),
            pltpu.SMEM(active.shape, jnp.int32),
            pltpu.SMEM((per,), jnp.int32),
            pltpu.VMEM(((n + 7) // 8 * 8, LANES), jnp.int32),
            pltpu.VMEM((n, 1, LANES), jnp.int32),
            pltpu.VMEM((n, 1, LANES), jnp.int32),
            pltpu.SMEM((n, 1, LANES), jnp.int32),
            dma((n_z + 5,)),
            dma((2, 2, n_c)),
            dma((2, 2, n_c)),
            dma(()),
            dma(()),
            dma(()),
            dma(()),
            dma(()),
            dma((2,)),
            dma((n_z + 1,)),
        ],
        compiler_params=pltpu.CompilerParams(
            collective_id=0, has_side_effects=True, vmem_limit_bytes=60 * 2**20
        ),
    )(
        wave_prev, wave_now, velocity, source, active, plan
    )
    first, second, image = pl.pallas_call(
        finish,
        out_shape=(
            jax.ShapeDtypeStruct((cx, ny, nz), f32),
            jax.ShapeDtypeStruct((cx, ny, nz), f32),
            jax.ShapeDtypeStruct((per, 32, LANES), f32),
        ),
        in_specs=[smem, free, free, free, free],
        out_specs=(hbm, hbm, hbm),
        scratch_shapes=[
            pltpu.VMEM((cx, ny, nz), f32),
            pltpu.VMEM((cx, ny, nz), f32),
            pltpu.VMEM((n * cap, 32, LANES), f32),
            pltpu.VMEM((per, 32, LANES), f32),
            pltpu.VMEM((per, 32, LANES), f32),
            dma((10,)),
        ],
        compiler_params=pltpu.CompilerParams(vmem_limit_bytes=60 * 2**20),
    )(place, first, second, incoming, image_in.reshape(per, 32, LANES))
    return first, second, image.reshape(image_in.shape)


def solution(mesh):
    lead = ("shot", "col")
    in_specs = (
        P(lead, None, None),
        P(lead, None, None),
        P(lead, None, None),
        P(None, lead, None, None),
        P(None, lead),
        P(lead),
        P(lead, None, None, None),
    )
    out_specs = (P(lead, None, None), P(lead, None, None), P(lead, None, None, None))
    return jax.shard_map(shards, mesh=mesh, in_specs=in_specs, out_specs=out_specs, check_vma=False)
```

```python
import functools

import jax
import jax.numpy as jnp
from jax import lax
from jax.experimental import pallas as pl
from jax.experimental.pallas import tpu as pltpu
from jax.sharding import PartitionSpec as P

COEF = (-205.0 / 72.0, 8.0 / 5.0, -1.0 / 5.0, 8.0 / 315.0, -1.0 / 560.0)
MESH = pl.DeviceIdType.MESH
R = 4
PAD = 8
CH = 16
LANES = 128


def flipped(me, k, bits):
    out = me
    for b in range(bits):
        out = out + ((k // 2**b) % 2) * (2**b) * (1 - 2 * ((me // 2**b) % 2))
    return out


def kernel(
    n, cap, prev_h, now_h, vel_h, src_h, active_h, plan_h,
    first_h, second_h, incoming, place_v,
    x1, x2, acc, prev_v, vel_v, src_v, second_v, bricks, outgoing, active_s, plan_s, want_2d, want_v, asked_v, asked_s,
    in_sem, halo_send, halo_recv, ask_send, ask_recv, ask_copy, a2a_send, a2a_recv, keep_sem, out_sem,
):
    me = lax.axis_index("col")
    cx, ny, nz = prev_h.shape
    n_c, n_z = ny // CH, nz // LANES
    bits = (n - 1).bit_length()

    def zero_rows(x, _):
        for j in range(n_z):
            for buf in (x1, x2):
                buf[R + x, j, 0:PAD, :] = jnp.zeros((PAD, LANES), jnp.float32)
                buf[R + x, j, PAD + ny : PAD + ny + PAD, :] = jnp.zeros((PAD, LANES), jnp.float32)
        return 0

    own = pl.ds(R, cx)
    body = pl.ds(PAD, ny)
    load_now = [
        pltpu.make_async_copy(
            now_h.at[:, :, pl.ds(j * LANES, LANES)], x1.at[own, j, body, :], in_sem.at[j]
        )
        for j in range(n_z)
    ]
    for copy in load_now:
        copy.start()
    load_plan = pltpu.make_async_copy(plan_h, plan_s, in_sem.at[n_z + 3])
    load_active = pltpu.make_async_copy(active_h, active_s, in_sem.at[n_z + 4])
    load_plan.start()
    load_active.start()
    load_prev = pltpu.make_async_copy(prev_h, prev_v, in_sem.at[n_z])
    load_vel = pltpu.make_async_copy(vel_h, vel_v, in_sem.at[n_z + 1])
    load_src = pltpu.make_async_copy(src_h, src_v, in_sem.at[n_z + 2])
    for copy in (load_prev, load_vel, load_src):
        copy.start()

    barrier = pltpu.get_barrier_semaphore()

    def greet(k, _):
        pl.semaphore_signal(
            barrier, inc=1, device_id={"col": lax.rem(me + k, n)}, device_id_type=MESH
        )
        return 0

    lax.fori_loop(1, n, greet, 0)

    lax.fori_loop(0, cx, zero_rows, 0)

    def zero_halo(start):
        def plane(x, _):
            for buf in (x1, x2):
                for j in range(n_z):
                    buf[start + x, j, PAD : PAD + ny, :] = jnp.zeros((ny, LANES), jnp.float32)
            return 0

        lax.fori_loop(0, R, plane, 0)

    @pl.when(me == 0)
    def _():
        zero_halo(0)

    @pl.when(me == n - 1)
    def _():
        zero_halo(R + cx)

    for copy in load_now:
        copy.wait()
    pl.semaphore_wait(barrier, n - 1)

    def halo(buf, step, side, c):
        rows = pl.ds(PAD + c * CH, CH)
        source, landing = ((cx, 0), (R, R + cx))[side]
        target = (lax.rem(me + 1, n), lax.rem(me + n - 1, n))[side]
        return pltpu.make_async_remote_copy(
            src_ref=buf.at[pl.ds(source, R), :, rows, :],
            dst_ref=buf.at[pl.ds(landing, R), :, rows, :],
            send_sem=halo_send.at[step, side, c],
            recv_sem=halo_recv.at[step, side, c],
            device_id={"col": target},
            device_id_type=MESH,
        )

    def send_halo(buf, step, c):
        @pl.when(me < n - 1)
        def _():
            halo(buf, step, 0, c).start()

        @pl.when(me > 0)
        def _():
            halo(buf, step, 1, c).start()

    def sent_halo(buf, step, c):
        @pl.when(me < n - 1)
        def _():
            halo(buf, step, 0, c).wait_send()

        @pl.when(me > 0)
        def _():
            halo(buf, step, 1, c).wait_send()

    def take_halo(buf, step, c):
        @pl.when(me > 0)
        def _():
            halo(buf, step, 0, c).wait_recv()

        @pl.when(me < n - 1)
        def _():
            halo(buf, step, 1, c).wait_recv()

    for c in range(n_c):
        send_halo(x1, 0, c)

    load_plan.wait()
    load_active.wait()
    per = plan_s.shape[0]
    slot = lax.broadcasted_iota(jnp.int32, (8, LANES), 1)
    zero = jnp.zeros((8, LANES), jnp.int32)

    def spread(s, carry):
        anchor, local = carry
        device = lax.div(plan_s[s], per)
        here = slot == s
        return jnp.where(here, device, anchor), jnp.where(here, plan_s[s] - device * per, local)

    anchor, local = lax.fori_loop(0, per, spread, (zero - 1, zero), unroll=8)

    def count(s, rank):
        device = lax.div(plan_s[s], per)
        return rank + jnp.where((slot > s) & (anchor == device), 1, 0)

    rank = lax.fori_loop(0, per, count, zero, unroll=8)
    place_v[...] = (anchor * cap + rank)[:1]

    def table(i, _):
        device = lax.broadcasted_iota(jnp.int32, (8, LANES), 0) + 8 * i
        rows = zero
        for r in range(cap):
            hit = (anchor == device) & (rank == r)
            pick = jnp.sum(jnp.where(hit, local, 0), axis=1, keepdims=True)
            rows = jnp.where(slot == r, pick, rows)
        want_2d[pl.ds(pl.multiple_of(8 * i, 8), 8), :] = rows
        return 0

    lax.fori_loop(0, (n + 7) // 8, table, 0)

    def lay(k, _):
        want_v[k] = want_2d[pl.ds(k, 1), :]
        return 0

    lax.fori_loop(0, n, lay, 0)

    def ask(k):
        target = lax.rem(me + k, n)
        return pltpu.make_async_remote_copy(
            src_ref=want_v.at[target],
            dst_ref=asked_v.at[me],
            send_sem=ask_send,
            recv_sem=ask_recv,
            device_id={"col": target},
            device_id_type=MESH,
        )

    def start_ask(k, _):
        ask(k).start()
        return 0

    lax.fori_loop(1, n, start_ask, 0)
    asked_v[me] = want_v[me]

    lane = lax.broadcasted_iota(jnp.int32, (CH, LANES), 1)
    row = lax.broadcasted_iota(jnp.int32, (CH, LANES), 0)

    def along_yz(buf, chunks):
        def plane(x, _):
            for c in chunks:
                tiles = [buf[R + x, j, PAD + c * CH : PAD + (c + 1) * CH, :] for j in range(n_z)]
                for j in range(n_z):
                    total = (3.0 * COEF[0]) * tiles[j]
                    for r in range(1, R + 1):
                        at = PAD + c * CH
                        pair = buf[R + x, j, at + r : at + r + CH, :] + buf[R + x, j, at - r : at - r + CH, :]
                        up = pltpu.roll(tiles[j], LANES - r, 1)
                        down = pltpu.roll(tiles[j], r, 1)
                        after = pltpu.roll(tiles[j + 1], LANES - r, 1) if j + 1 < n_z else 0.0
                        before = pltpu.roll(tiles[j - 1], r, 1) if j > 0 else 0.0
                        pair = pair + jnp.where(lane < LANES - r, up, after)
                        pair = pair + jnp.where(lane < r, before, down)
                        total = total + COEF[r] * pair
                    acc[x, j, c * CH : (c + 1) * CH, :] = total
            return 0

        lax.fori_loop(0, cx, plane, 0)

    def mask(t, c, j):
        per = CH // 4
        flags = [active_s[t, (c * per + i) * n_z + j].astype(jnp.float32) for i in range(per)]
        out = jnp.full((CH, LANES), flags[per - 1], jnp.float32)
        for i in range(per - 2, -1, -1):
            out = jnp.where(row < 4 * (i + 1), flags[i], out)
        return out

    def following(buf, x, c, j, before, flag):
        rows = slice(PAD + c * CH, PAD + (c + 1) * CH)
        total = acc[x, j, c * CH : (c + 1) * CH, :]
        for r in range(1, R + 1):
            total = total + COEF[r] * (buf[R + x + r, j, rows, :] + buf[R + x - r, j, rows, :])
        here = buf[R + x, j, rows, :]
        speed = vel_v[x, c * CH : (c + 1) * CH, j * LANES : (j + 1) * LANES]
        return here, flag * (2.0 * here - before + speed * total)

    even = lax.rem(me, 2) == 0

    def take_near(buf, step, c):
        @pl.when(jnp.logical_not(even))
        def _():
            halo(buf, step, 0, c).wait_recv()

        @pl.when(even & (me < n - 1))
        def _():
            halo(buf, step, 1, c).wait_recv()

    def take_other(buf, step, c):
        @pl.when(even & (me > 0))
        def _():
            halo(buf, step, 0, c).wait_recv()

        @pl.when(jnp.logical_not(even) & (me < n - 1))
        def _():
            halo(buf, step, 1, c).wait_recv()

    along_yz(x1, range(n_c))
    half = cx // 2
    base_near = half * (1 - lax.rem(me, 2))

    bases = (base_near, half - base_near)

    def second_half(phase, take, chunks):
        base = bases[phase]
        for c in chunks:
            take(x2, 1, c)
            flags = [mask(1, c, j) for j in range(n_z)]

            def pair(p, _):
                for j in range(n_z):
                    gains = []
                    for i in range(2):
                        x = base + 2 * p + i
                        before = x1[R + x, j, PAD + c * CH : PAD + (c + 1) * CH, :]
                        here, new = following(x2, x, c, j, before, flags[j])
                        spot = (slice(c * CH, (c + 1) * CH), slice(j * LANES, (j + 1) * LANES))
                        second_v[(x,) + spot] = new
                        gains.append(
                            src_v[(0, x) + spot].astype(jnp.float32) * here
                            + src_v[(1, x) + spot].astype(jnp.float32) * new
                        )
                    for h in range(CH // 8):
                        a, b = (g[h * 8 : (h + 1) * 8, :] for g in gains)
                        low = row[:8] < 4
                        first = jnp.where(low, a, pltpu.roll(b, 4, 0))
                        other = jnp.where(low, pltpu.roll(a, 4, 0), b)
                        yb = c * (CH // 4) + 2 * h
                        for i, value in enumerate((first, other)):
                            at = (yb + i) * n_z + j
                            bricks[phase, at, pl.ds(pl.multiple_of(8 * p, 8), 8), :] = value
                return 0

            lax.fori_loop(0, half // 2, pair, 0)

    pltpu.make_async_copy(
        asked_v.at[pl.ds(0, n - 1)], asked_v.at[pl.ds(0, n - 1)], ask_recv
    ).wait()
    to_scalar = pltpu.make_async_copy(asked_v, asked_s, ask_copy)
    to_scalar.start()
    load_prev.wait()
    load_vel.wait()
    for c in range(n_c):
        take_halo(x1, 0, c)
        flags = [mask(0, c, j) for j in range(n_z)]

        def plane(x, _):
            for j in range(n_z):
                before = prev_v[x, c * CH : (c + 1) * CH, j * LANES : (j + 1) * LANES]
                _, new = following(x1, x, c, j, before, flags[j])
                x2[R + x, j, PAD + c * CH : PAD + (c + 1) * CH, :] = new
            return 0

        lax.fori_loop(0, cx, plane, 0)
        send_halo(x2, 1, c)
        if c > 0:
            along_yz(x2, [c - 1])
        if c == 1:
            load_src.wait()
        if c > 1:
            second_half(0, take_near, [c - 2])
    along_yz(x2, [n_c - 1])
    second_half(0, take_near, [n_c - 2, n_c - 1])

    def pack(phase, k, target):
        for r in range(cap):
            outgoing[phase, k * cap + r] = bricks[phase, asked_s[target, 0, r]]

    def landing(base):
        rows = pl.ds(pl.multiple_of(base * 4, 16), half * 4)
        return incoming.at[pl.ds(me * cap, cap), rows, :]

    def give(phase, k):
        target = flipped(me, k, bits) if n == 2**bits else lax.rem(me + k, n)
        pack(phase, k, target)
        pltpu.make_async_remote_copy(
            src_ref=outgoing.at[phase, pl.ds(k * cap, cap)],
            dst_ref=landing(bases[phase]),
            send_sem=a2a_send,
            recv_sem=a2a_recv,
            device_id={"col": target},
            device_id_type=MESH,
        ).start()

    def give_group(phase, start, top, shift):
        def one(i, _):
            give(phase, top + (i // 2) * 4 + shift + i % 2)
            return 0

        lax.fori_loop(start, n // 4, one, 0)

    def give_all(phase):
        def one(i, _):
            give(phase, i)
            return 0

        lax.fori_loop(1, n, one, 0)

    grouped = n == 2**bits and n >= 8
    to_scalar.wait()
    if grouped:
        give_group(0, 0, n // 2, 0)
        give_group(0, 0, n // 2, 2)
        give_group(0, 1, 0, 0)
    else:
        give_all(0)
    store_first = [
        pltpu.make_async_copy(
            x2.at[own, j, body, :], first_h.at[:, :, pl.ds(j * LANES, LANES)], out_sem.at[j]
        )
        for j in range(n_z)
    ]
    for copy in store_first:
        copy.start()
    second_half(1, take_other, range(n_c))
    if grouped:
        give_group(1, 0, n // 2, 0)
        give_group(1, 0, n // 2, 2)
        give_group(0, 0, 0, 2)
        give_group(1, 0, 0, 2)
        give_group(1, 1, 0, 0)
    else:
        give_all(1)

    store_second = pltpu.make_async_copy(second_v, second_h, out_sem.at[n_z])
    store_second.start()
    keeps = []
    for phase in range(2):
        pack(phase, 0, me)
        keep = pltpu.make_async_copy(
            outgoing.at[phase, pl.ds(0, cap)], landing(bases[phase]), keep_sem.at[phase]
        )
        keep.start()
        keeps.append(keep)

    whole = pl.ds(cap, (n - 1) * cap)
    pltpu.make_async_copy(incoming.at[whole], incoming.at[whole], a2a_recv).wait()

    for c in range(n_c):
        sent_halo(x1, 0, c)
        sent_halo(x2, 1, c)
    pltpu.make_async_copy(
        want_v.at[pl.ds(0, n - 1)], want_v.at[pl.ds(0, n - 1)], ask_send
    ).wait()
    pltpu.make_async_copy(outgoing.at[:, whole], outgoing.at[:, whole], a2a_send).wait()
    for copy in store_first + [store_second] + keeps:
        copy.wait()


def finish(
    place_s, first_h, second_h, incoming_h, img_h, first_out, second_out, image_out,
    first_v, second_v, incoming, img_v, sum_v, sem,
):
    waves = [
        pltpu.make_async_copy(first_h, first_v, sem.at[8]),
        pltpu.make_async_copy(second_h, second_v, sem.at[9]),
    ]
    loads = [
        pltpu.make_async_copy(incoming_h, incoming, sem.at[6]),
        pltpu.make_async_copy(img_h, img_v, sem.at[7]),
    ]
    for copy in waves + loads:
        copy.start()
    copies = [
        pltpu.make_async_copy(first_v, first_out, sem.at[0]),
        pltpu.make_async_copy(second_v, second_out, sem.at[1]),
    ]
    for load, copy in zip(waves, copies):
        load.wait()
        copy.start()
    per = img_v.shape[0]
    parts = 4 if per % 4 == 0 else 1
    step = per // parts
    for copy in loads:
        copy.wait()
    for q in range(parts):

        def add(i, _):
            s = q * step + i
            sum_v[s] = img_v[s] + incoming[place_s[0, s]]
            return 0

        lax.fori_loop(0, step, add, 0)
        span = pl.ds(q * step, step)
        copy = pltpu.make_async_copy(sum_v.at[span], image_out.at[span], sem.at[2 + q])
        copy.start()
        copies.append(copy)
    for copy in copies:
        copy.wait()


def shards(wave_prev, wave_now, velocity, source, active, plan, image_in):
    cx, ny, nz = wave_now.shape
    n = lax.axis_size("col")
    per = plan.shape[0]
    cap = (per + n - 1) // n
    n_c, n_z = ny // CH, nz // LANES

    f32 = jnp.float32
    hbm = pl.BlockSpec(memory_space=pltpu.HBM)
    free = pl.BlockSpec(memory_space=pl.ANY)
    smem = pl.BlockSpec(memory_space=pltpu.SMEM)
    vmem = pl.BlockSpec(memory_space=pltpu.VMEM)
    assert per <= LANES
    wide = (cx + 2 * R, n_z, ny + 2 * PAD, LANES)
    dma = pltpu.SemaphoreType.DMA
    first, second, incoming, place = pl.pallas_call(
        functools.partial(kernel, n, cap),
        out_shape=(
            jax.ShapeDtypeStruct((cx, ny, nz), f32),
            jax.ShapeDtypeStruct((cx, ny, nz), f32),
            jax.ShapeDtypeStruct((n * cap, 32, LANES), f32),
            jax.ShapeDtypeStruct((1, LANES), jnp.int32),
        ),
        in_specs=[hbm] * 6,
        out_specs=(free, free, free, vmem),
        scratch_shapes=[
            pltpu.VMEM(wide, f32),
            pltpu.VMEM(wide, f32),
            pltpu.VMEM((cx, n_z, ny, LANES), f32),
            pltpu.VMEM((cx, ny, nz), f32),
            pltpu.VMEM((cx, ny, nz), f32),
            pltpu.VMEM((2, cx, ny, nz), jnp.bfloat16),
            pltpu.VMEM((cx, ny, nz), f32),
            pltpu.VMEM((2, per, 16, LANES), f32),
            pltpu.VMEM((2, n * cap, 16, LANES), f32),
            pltpu.SMEM(active.shape, jnp.int32),
            pltpu.SMEM((per,), jnp.int32),
            pltpu.VMEM(((n + 7) // 8 * 8, LANES), jnp.int32),
            pltpu.VMEM((n, 1, LANES), jnp.int32),
            pltpu.VMEM((n, 1, LANES), jnp.int32),
            pltpu.SMEM((n, 1, LANES), jnp.int32),
            dma((n_z + 5,)),
            dma((2, 2, n_c)),
            dma((2, 2, n_c)),
            dma(()),
            dma(()),
            dma(()),
            dma(()),
            dma(()),
            dma((2,)),
            dma((n_z + 1,)),
        ],
        compiler_params=pltpu.CompilerParams(
            collective_id=0, has_side_effects=True, vmem_limit_bytes=60 * 2**20
        ),
    )(
        wave_prev, wave_now, velocity, source, active, plan
    )
    first, second, image = pl.pallas_call(
        finish,
        out_shape=(
            jax.ShapeDtypeStruct((cx, ny, nz), f32),
            jax.ShapeDtypeStruct((cx, ny, nz), f32),
            jax.ShapeDtypeStruct((per, 32, LANES), f32),
        ),
        in_specs=[smem, free, free, free, free],
        out_specs=(hbm, hbm, hbm),
        scratch_shapes=[
            pltpu.VMEM((cx, ny, nz), f32),
            pltpu.VMEM((cx, ny, nz), f32),
            pltpu.VMEM((n * cap, 32, LANES), f32),
            pltpu.VMEM((per, 32, LANES), f32),
            pltpu.VMEM((per, 32, LANES), f32),
            dma((10,)),
        ],
        compiler_params=pltpu.CompilerParams(vmem_limit_bytes=60 * 2**20),
    )(place, first, second, incoming, image_in.reshape(per, 32, LANES))
    return first, second, image.reshape(image_in.shape)


def solution(mesh):
    lead = ("shot", "col")
    in_specs = (
        P(lead, None, None),
        P(lead, None, None),
        P(lead, None, None),
        P(None, lead, None, None),
        P(None, lead),
        P(lead),
        P(lead, None, None, None),
    )
    out_specs = (P(lead, None, None), P(lead, None, None), P(lead, None, None, None))
    return jax.shard_map(shards, mesh=mesh, in_specs=in_specs, out_specs=out_specs, check_vma=False)
```
